128 devices in a mesh: dp: 4 (over z), expert: 32 (over y, x, core).
Axes of the slice: x: 4, y: 4, z: 4, core: 2. Of those that a mesh axis runs over, the one named last changes fastest.
Arguments:
- tokens: bfloat16 [16384, 3584], P(('dp', 'expert')), may hold values from -6 to 6
- cotangent: bfloat16 [16384, 3584], P(('dp', 'expert')), may hold values from -6 to 6
- gates: bfloat16 [16384, 2], P(('dp', 'expert')), may hold values from 0.099609375 to 1
- expert_ids: int32 [16384, 2], P(('dp', 'expert')), may hold values from 0 to 31, all different within a row; in each aligned block of 128 rows (0 to 127, 128 to 255, ...) at most 10 rows name the same one
- w_gate: bfloat16 [32, 3584, 1024], P('expert', 'dp'), may hold values from -0.09375 to 0.09375
- w_up: bfloat16 [32, 3584, 1024], P('expert', 'dp'), may hold values from -0.09375 to 0.09375
- w_down: bfloat16 [32, 1024, 3584], P('expert', None, 'dp'), may hold values from -0.1875 to 0.1875
- hot_experts: int32 [32], replicated, may hold values from 0 to 31, each once
- copy_counts: int32 [128, 32], P(('dp', 'expert')), may hold values from 0 to 2
Outputs:
- d_tokens: bfloat16 [16384, 3584], P(('dp', 'expert'))
- d_gates: bfloat16 [16384, 2], P(('dp', 'expert'))
- grad_gate: bfloat16 [32, 3584, 1024], P('expert', 'dp')
- grad_up: bfloat16 [32, 3584, 1024], P('expert', 'dp')
- grad_down: bfloat16 [32, 1024, 3584], P('expert', None, 'dp')
- loads: float32 [4, 32], P('dp', 'expert')
The draws below stay inside these ranges and needn't reach their ends.
Inputs may be any that keep to these rules, and one draw needn't show every extreme that they name: `expert_ids`: in the rows of one device no expert is named by more than 10 rows, a bound that some block reaches. `hot_experts`: each expert exactly once.
All inputs are finite; a program needn't handle non-finite values.
Results may differ from the reference program's by a relative error of at most 0.03.
Values may be sent and summed in bfloat16 or wider, within the bound.
No kernel may reach another device: no remote copies, remote signals or barrier semaphores. Data moves between devices by JAX's collectives and lax.ppermute only.
A program may use at most 128 MiB of HBM per device.

```python
import math
import jax
import jax.numpy as jnp
import numpy as np
from jax import lax

D = 3584
FS = 1024
TOK_DEV = 128
TOPK = 2
CAPC = 2
EXPERTS = 32
NREP = 32
TOKENS = 16384
MOST = 10
N_DP = 4
N_EXPERT = 32


def touch_ends(values, own_key, smallest, largest):
    place = [jax.random.randint(jax.random.fold_in(own_key, axis), (), 0, length) for axis, length in enumerate(values.shape)]
    widest = values.shape.index(max(values.shape))
    neighbour = place[:widest] + [(place[widest] + 1) % values.shape[widest]] + place[widest + 1:]
    return values.at[tuple(place)].set(smallest).at[tuple(neighbour)].set(largest)


def shard_levels(rng, dims, cuts, smallest, largest):
    gain, own = 1.0, jax.random.fold_in(rng, 6)
    for dim, shards_of in cuts:
        draws = jnp.exp(jax.random.uniform(jax.random.fold_in(own, dim), (shards_of,), jnp.float32, smallest / len(cuts), largest / len(cuts)))
        gain = gain * jnp.repeat(draws, dims[dim] // shards_of).reshape([-1 if axis == dim else 1 for axis in range(len(dims))])
    return gain


def assign_block(own_key, own, number, rows, count, top, most, skew):
    ranking = jax.random.permutation(own_key, count)
    heavy_load, ordinary = shares(count, rows * top, most, skew, True), shares(count, rows * top, most, skew, False)
    places = jnp.arange(count)

    def named(tallies, offset_by):
        used = int((tallies > 0).sum())
        fixed = max(1, used // 4)
        passed = fixed + (places - fixed + offset_by * (used - fixed)) % max(1, count - fixed)
        return jnp.zeros((count,), jnp.int32).at[ranking[jnp.where(places < fixed, places, passed)]].set(jnp.asarray(tallies, jnp.int32))

    tallies = jnp.where(number % 4 == 0, named(heavy_load, number // 4), named(ordinary, number - number // 4 - 1))
    mixed = jax.random.permutation(jax.random.fold_in(own, 3), count)
    donor, receiver = mixed[0:count // 2 * 2:2], mixed[1:count // 2 * 2:2]
    margin = jnp.minimum(tallies[donor] - 1, most - tallies[receiver]) // 2
    margin = jnp.where((donor == ranking[0]) | (receiver == ranking[0]) | (tallies[receiver] == 0), 0, jnp.maximum(margin, 0))
    passed = jax.random.randint(jax.random.fold_in(own, 4), (count // 2,), 0, 1 << 20) % (margin + 1)
    tallies = tallies.at[donor].add(-passed).at[receiver].add(passed)
    members = jnp.searchsorted(jnp.cumsum(tallies), jnp.arange(rows * top), side="right").astype(jnp.int32)
    listing = members.reshape(top, rows).T
    listing = listing[jax.random.permutation(jax.random.fold_in(own, 1), rows)]
    offset_by = jax.random.randint(jax.random.fold_in(own, 2), (rows, 1), 0, top)
    return jnp.take_along_axis(listing, (jnp.arange(top)[None, :] + offset_by) % top, axis=1)


def shares(count, total, bound, slope, full):
    weights = [(1 << 20) // math.isqrt(standing ** slope) + 1 for standing in range(1, count + 1)]
    largest = bound if full else min(bound, max(-(-total // count), total * weights[0] // sum(weights)))
    least = 1 if total - largest >= count - 1 else 0
    holding, rest = [largest] + [least] * (count - 1), total - largest - least * (count - 1)
    while rest > 0:
        free = [i for i in range(1, count) if holding[i] < largest] or [i for i in range(1, count) if holding[i] < bound]
        whole, budget = sum([weights[i] for i in free]), rest
        for i in free:
            more = min(bound - holding[i], max(1, budget * weights[i] // whole), rest)
            holding[i] = holding[i] + more
            rest = rest - more
    return np.array(holding)


def scatter_about(rng, shape, width, most, cuts=(), kind=jnp.bfloat16):
    gain = shard_levels(rng, shape, cuts, -0.22, 0.18) if cuts else 1.0
    values = jax.random.normal(rng, shape, jnp.float32) * width * gain
    return jnp.minimum(jnp.maximum(values, -most), most).astype(kind)


def setup_inputs(seed: int = 0) -> dict:
    seeds = jax.random.split(jax.random.key(seed), 10)
    tokens = scatter_about(seeds[0], (TOKENS, D), 1.0, 6.0, ((0, 128),))
    cotangent = scatter_about(seeds[1], (TOKENS, D), 1.0, 6.0, ((0, 128),))
    gates = jnp.clip(jnp.exp(math.log(1.0) - 2.306499 * jax.random.uniform(seeds[2], (TOKENS, TOPK), jnp.float32) ** shard_levels(seeds[2], (TOKENS, TOPK), ((0, 128),), -0.2, 0.2)), 0.099609375, 1.0).astype(jnp.bfloat16)
    expert_ids_keys = jax.random.split(jax.random.fold_in(seeds[3], 1), TOKENS // TOK_DEV)
    expert_ids_turns = jax.random.permutation(jax.random.fold_in(seeds[3], 3), TOKENS // TOK_DEV)
    expert_ids = jax.vmap(lambda own, number: assign_block(jax.random.fold_in(seeds[3], 2), own, number, TOK_DEV, EXPERTS, TOPK, MOST, 1))(expert_ids_keys, expert_ids_turns).reshape((TOKENS, TOPK))
    w_gate = scatter_about(seeds[4], (EXPERTS, D, FS), D ** -0.5, 0.09375, ((0, 32), (1, 4)))
    w_up = scatter_about(seeds[5], (EXPERTS, D, FS), D ** -0.5, 0.09375, ((0, 32), (1, 4)))
    w_down = scatter_about(seeds[6], (EXPERTS, FS, D), FS ** -0.5, 0.1875, ((0, 32), (2, 4)))
    hot_experts = jax.random.permutation(seeds[7], EXPERTS).astype(jnp.int32)
    copy_counts = touch_ends(jax.random.randint(seeds[8], (N_DP * N_EXPERT, NREP), 0, CAPC + 1), jax.random.fold_in(seeds[8], 1), 0, CAPC).astype(jnp.int32)
    return dict(tokens=tokens, cotangent=cotangent, gates=gates, expert_ids=expert_ids, w_gate=w_gate, w_up=w_up, w_down=w_down, hot_experts=hot_experts, copy_counts=copy_counts)


def routing_plan(picked, asked_rows, hot_list, expert_count):
    columns = jnp.arange(expert_count, dtype=jnp.int32)
    onehot = (picked[:, None] == columns[None, :]).astype(jnp.int32)
    earlier = jnp.cumsum(onehot, axis=0) - onehot
    order_rank = lax.optimization_barrier(jnp.sum(earlier * onehot, axis=1))
    named_count = lax.optimization_barrier(jnp.sum(onehot, axis=0))
    hot_match = (hot_list[:, None] == columns[None, :]).astype(jnp.int32)
    wanted = lax.optimization_barrier(jnp.sum(hot_match * asked_rows[:, None], axis=0))
    used_rows = jnp.minimum(wanted, named_count)
    used_per_row = lax.optimization_barrier(jnp.sum(onehot * used_rows[None, :], axis=1))
    to_copy = order_rank < used_per_row
    return (order_rank, named_count, used_rows, used_per_row, to_copy)

def quarter_sum(partials):
    rounded = lax.optimization_barrier(partials.astype(jnp.bfloat16))
    return lax.optimization_barrier(jnp.sum(rounded.astype(jnp.float32), axis=0))

def expert_pass(rows_in, rows_cot, gate_col, slab_gate, slab_up, slab_down, gate_scale):
    row_total = rows_in.shape[0]
    quarter = D // N_DP
    contract = (((1,), (1,)), ((), ()))
    split_in = rows_in.astype(jnp.float32).reshape(row_total, N_DP, quarter)
    gate_pre = quarter_sum(jnp.einsum('rjd,jdf->jrf', split_in, slab_gate.astype(jnp.float32).reshape(N_DP, quarter, FS)))
    up_pre = quarter_sum(jnp.einsum('rjd,jdf->jrf', split_in, slab_up.astype(jnp.float32).reshape(N_DP, quarter, FS)))
    sigmoid = jax.nn.sigmoid(gate_pre)
    active = gate_pre * sigmoid
    hidden = (active * up_pre).astype(jnp.bfloat16)
    output = jnp.dot(hidden, slab_down, preferred_element_type=jnp.float32)
    cot_float = rows_cot.astype(jnp.float32)
    gate_parts = lax.optimization_barrier(jnp.sum((cot_float * output).reshape(row_total, N_DP, quarter), axis=2)).T
    d_gate = (quarter_sum(gate_parts) * gate_scale).astype(jnp.bfloat16)
    d_output = (gate_col.astype(jnp.float32)[:, None] * cot_float).astype(jnp.bfloat16)
    split_out = d_output.astype(jnp.float32).reshape(row_total, N_DP, quarter)
    d_hidden = quarter_sum(jnp.einsum('rjd,fjd->jrf', split_out, slab_down.astype(jnp.float32).reshape(FS, N_DP, quarter)))
    d_gate_pre = (d_hidden * up_pre * sigmoid * (1.0 + gate_pre * (1.0 - sigmoid))).astype(jnp.bfloat16)
    d_up_pre = (d_hidden * active).astype(jnp.bfloat16)
    d_rows = lax.dot_general(d_gate_pre, slab_gate, contract, preferred_element_type=jnp.float32)
    d_rows = d_rows + lax.dot_general(d_up_pre, slab_up, contract, preferred_element_type=jnp.float32)
    return (d_rows.astype(jnp.bfloat16), d_gate, (rows_in, hidden, d_output, d_gate_pre, d_up_pre))

def weight_terms(saved_rows, keep_mask, grad_scale):
    rows_in, hidden, d_output, d_gate_pre, d_up_pre = saved_rows
    keep_col = keep_mask.astype(d_output.dtype)[:, None]
    outer_dims = (((0,), (0,)), ((), ()))
    grad_g = lax.dot_general(rows_in, d_gate_pre * keep_col, outer_dims, preferred_element_type=jnp.float32)
    grad_u = lax.dot_general(rows_in, d_up_pre * keep_col, outer_dims, preferred_element_type=jnp.float32)
    grad_d = lax.dot_general(hidden, d_output * keep_col, outer_dims, preferred_element_type=jnp.float32)
    return ((grad_g * grad_scale).astype(jnp.bfloat16), (grad_u * grad_scale).astype(jnp.bfloat16), (grad_d * grad_scale).astype(jnp.bfloat16))

def reference(tokens, cotangent, gates, expert_ids, w_gate, w_up, w_down, hot_experts, copy_counts):
    devices = N_DP * N_EXPERT
    row_count = TOK_DEV * TOPK
    half_way = N_EXPERT // 2
    capacity = MOST + CAPC
    all_rows = TOKENS * TOPK
    grad_scale = 1.0 / math.sqrt(row_count * N_DP)
    gate_scale = 1.0 / math.sqrt(D)
    chosen = expert_ids.reshape(devices, row_count)
    order_rank, named_count, used_rows, used_per_row, to_copy = jax.vmap(lambda picked, asked_rows: routing_plan(picked, asked_rows, hot_experts, EXPERTS))(chosen, copy_counts)
    source = jnp.arange(devices, dtype=jnp.int32)[:, None]
    position = jnp.where(to_copy, MOST + order_rank, order_rank - used_per_row)
    flat_slot = (chosen * devices + source) * capacity + position
    slot_table = jnp.full((EXPERTS * devices * capacity,), all_rows, jnp.int32)
    slot_table = slot_table.at[flat_slot.reshape(-1)].set(jnp.arange(all_rows, dtype=jnp.int32))
    gate_flat = gates.reshape(all_rows)
    block_size = devices * capacity
    region = (jnp.arange(block_size, dtype=jnp.int32) % capacity >= MOST).astype(jnp.float32)

    def visit_expert(carry, expert_at):
        d_tok, d_gate_all, acc_g, acc_u, acc_d = carry
        slot_rows = lax.dynamic_slice_in_dim(slot_table, expert_at * block_size, block_size)
        token_index = slot_rows // TOPK
        rows_in = jnp.take(tokens, token_index, axis=0, mode='fill', fill_value=0)
        rows_cot = jnp.take(cotangent, token_index, axis=0, mode='fill', fill_value=0)
        gate_col = jnp.take(gate_flat, slot_rows, axis=0, mode='fill', fill_value=0)
        slab_gate = lax.dynamic_index_in_dim(w_gate, expert_at, 0, keepdims=False)
        slab_up = lax.dynamic_index_in_dim(w_up, expert_at, 0, keepdims=False)
        slab_down = lax.dynamic_index_in_dim(w_down, expert_at, 0, keepdims=False)
        d_rows, d_gate, saved_rows = expert_pass(rows_in, rows_cot, gate_col, slab_gate, slab_up, slab_down, gate_scale)
        main_terms = weight_terms(saved_rows, 1.0 - region, grad_scale)
        copy_terms = weight_terms(saved_rows, region, grad_scale)
        d_tok = d_tok.at[token_index].add(d_rows.astype(jnp.float32), mode='drop')
        d_gate_all = d_gate_all.at[slot_rows].set(d_gate.astype(jnp.float32), mode='drop')
        acc_g = acc_g.at[expert_at].set(main_terms[0].astype(jnp.float32) + copy_terms[0].astype(jnp.float32))
        acc_u = acc_u.at[expert_at].set(main_terms[1].astype(jnp.float32) + copy_terms[1].astype(jnp.float32))
        acc_d = acc_d.at[expert_at].set(main_terms[2].astype(jnp.float32) + copy_terms[2].astype(jnp.float32))
        return ((d_tok, d_gate_all, acc_g, acc_u, acc_d), None)
    initial = (jnp.zeros((TOKENS, D), jnp.float32), jnp.zeros((all_rows,), jnp.float32), jnp.zeros((EXPERTS, D, FS), jnp.float32), jnp.zeros((EXPERTS, D, FS), jnp.float32), jnp.zeros((EXPERTS, FS, D), jnp.float32))
    finished, _ = lax.scan(visit_expert, initial, jnp.arange(EXPERTS, dtype=jnp.int32))
    d_tok, d_gate_all, acc_g, acc_u, acc_d = finished
    served = named_count - used_rows + jnp.roll(used_rows, half_way, axis=1)
    loads = lax.optimization_barrier(jnp.sum(served.reshape(N_DP, N_EXPERT, EXPERTS), axis=1)).astype(jnp.float32) / row_count
    return (d_tok.astype(jnp.bfloat16), d_gate_all.reshape(TOKENS, TOPK).astype(jnp.bfloat16), acc_g.astype(jnp.bfloat16), acc_u.astype(jnp.bfloat16), acc_d.astype(jnp.bfloat16), loads)
```

```python
import math

import jax
import jax.numpy as jnp
from jax import lax
from jax.sharding import PartitionSpec as P

MOST = 10


def routing_plan(picked, asked_rows, hot_list, expert_count):
    rows = picked.shape[0]
    place = jnp.arange(rows, dtype=jnp.int32)
    earlier = (picked[:, None] == picked[None, :]) & (place[None, :] < place[:, None])
    order_rank = jnp.sum(earlier.astype(jnp.int32), axis=1)
    columns = jnp.arange(expert_count, dtype=jnp.int32)
    onehot = (picked[:, None] == columns[None, :]).astype(jnp.int32)
    named_count = jnp.sum(onehot, axis=0)
    hot_match = (hot_list[:, None] == columns[None, :]).astype(jnp.int32)
    wanted = jnp.sum(hot_match * asked_rows[:, None], axis=0)
    used_rows = jnp.minimum(wanted, named_count)
    return order_rank, named_count, used_rows


def to_quarters(value, groups):
    rows, width = value.shape
    parts = value.reshape(rows, groups, width // groups).transpose(1, 0, 2)
    got = lax.all_to_all(parts, "dp", 0, 0, tiled=True)
    return got.reshape(groups * rows, width // groups)


def from_quarters(value, groups):
    rows, width = value.shape[0] // groups, value.shape[1]
    got = lax.all_to_all(value.reshape(groups, rows, width), "dp", 0, 0, tiled=True)
    return got.transpose(1, 0, 2).reshape(rows, groups * width)


def over_experts(value):
    return lax.all_to_all(value, "expert", 0, 0, tiled=True)


def shards(tokens, cotangent, gates, expert_ids, w_gate, w_up, w_down, hot_experts, copy_counts):
    model_width = tokens.shape[1]
    tok_dev, top_count = expert_ids.shape
    row_count = tok_dev * top_count
    groups = lax.axis_size("dp")
    servers = lax.axis_size("expert")
    group = lax.axis_index("dp")
    grad_scale = 1.0 / math.sqrt(row_count * groups)
    gate_scale = 1.0 / math.sqrt(model_width)
    per_pair = groups * MOST
    slots = servers * per_pair
    own_slots = slots // groups
    f32, bf16 = jnp.float32, jnp.bfloat16

    chosen = expert_ids.reshape(row_count)
    order_rank, named_count, used_rows = routing_plan(chosen, copy_counts[0], hot_experts, servers)
    slot_row = chosen * per_pair + group * MOST + order_rank
    plan = jnp.stack([slot_row.astype(f32), gates.reshape(row_count).astype(f32)])
    plan = lax.all_gather(plan, "dp", axis=0)
    tok_q = to_quarters(tokens, groups)
    cot_q = to_quarters(cotangent, groups)

    slot_of = plan[:, 0].astype(jnp.int32).reshape(groups * tok_dev, top_count)
    gate_of = plan[:, 1].reshape(groups * tok_dev, top_count)
    slot_ids = jnp.arange(slots, dtype=jnp.int32)[:, None]
    hits = [slot_ids == slot_of[None, :, k] for k in range(top_count)]
    dispatch = hits[0]
    for hit in hits[1:]:
        dispatch = dispatch | hit
    dispatch = dispatch.astype(bf16)
    slot_gate = sum(
        jnp.sum(jnp.where(hit, gate_of[None, :, k], 0.0), axis=1) for k, hit in enumerate(hits)
    )
    served = (named_count - used_rows + jnp.roll(used_rows, servers // 2)).astype(f32)
    small = jnp.concatenate([slot_gate.reshape(servers, per_pair), served[:, None]], axis=1)
    small = over_experts(small)
    load_here = jnp.sum(small[:, per_pair]) / row_count
    row_gate = small[:, :per_pair].reshape(slots)
    row_gate = lax.dynamic_slice_in_dim(row_gate, group * own_slots, own_slots)[:, None]

    send_in = jnp.dot(dispatch, tok_q, preferred_element_type=f32).astype(bf16)
    send_cot = jnp.dot(dispatch, cot_q, preferred_element_type=f32).astype(bf16)
    rows_in = over_experts(send_in)
    rows_cot = over_experts(send_cot)

    w_both = jnp.concatenate([w_gate[0], w_up[0]], axis=1)
    hidden_width = w_gate.shape[2]
    own_down = w_down[0]
    across = (((1,), (1,)), ((), ()))
    pre_part = jnp.dot(rows_in, w_both, preferred_element_type=f32).astype(bf16)
    pre = lax.psum_scatter(pre_part, "dp", scatter_dimension=0, tiled=True).astype(f32)
    back_part = lax.dot_general(rows_cot, own_down, across, preferred_element_type=f32).astype(bf16)
    back = lax.psum_scatter(back_part, "dp", scatter_dimension=0, tiled=True).astype(f32)

    gate_pre, up_pre = pre[:, :hidden_width], pre[:, hidden_width:]
    sigmoid = jax.nn.sigmoid(gate_pre)
    active = gate_pre * sigmoid
    hidden = active * up_pre
    d_gate_rows = jnp.sum(hidden * back, axis=1) * gate_scale
    d_hidden = row_gate * back
    d_gate_pre = d_hidden * up_pre * sigmoid * (1.0 + gate_pre * (1.0 - sigmoid))
    d_up_pre = d_hidden * active
    d_both = jnp.concatenate([d_gate_pre.astype(bf16), d_up_pre.astype(bf16)], axis=1)
    gated = (hidden * row_gate).astype(bf16)

    d_both = lax.all_gather(d_both, "dp", axis=0, tiled=True)
    gated = lax.all_gather(gated, "dp", axis=0, tiled=True)
    d_gate_all = lax.all_gather(d_gate_rows[None], "dp", axis=0, tiled=True)

    d_rows = lax.dot_general(d_both, w_both, across, preferred_element_type=f32).astype(bf16)
    back_rows = over_experts(d_rows)
    back_gate = over_experts(d_gate_all.reshape(servers, per_pair))

    outer = (((0,), (0,)), ((), ()))
    grad_both = [
        (lax.dot_general(rows_in, part, outer, preferred_element_type=f32) * grad_scale).astype(bf16)
        for part in (d_both[:, :hidden_width], d_both[:, hidden_width:])
    ]
    grad_down = lax.dot_general(gated, rows_cot, outer, preferred_element_type=f32)
    grad_down = (grad_down * grad_scale).astype(bf16)

    d_tok_q = lax.dot_general(dispatch, back_rows, outer, preferred_element_type=f32).astype(bf16)
    d_tokens = from_quarters(d_tok_q, groups)

    mine = lax.dynamic_slice_in_dim(back_gate, group * MOST, MOST, axis=1).reshape(1, servers * MOST)
    spot = chosen * MOST + order_rank
    match = spot[:, None] == jnp.arange(servers * MOST, dtype=jnp.int32)[None, :]
    d_gates = jnp.sum(jnp.where(match, mine, 0.0), axis=1).astype(bf16).reshape(tok_dev, top_count)
    return (
        d_tokens,
        d_gates,
        grad_both[0][None],
        grad_both[1][None],
        grad_down[None],
        load_here.reshape(1, 1),
    )


def solution(mesh):
    rows = P(("dp", "expert"), None)
    return jax.shard_map(
        shards,
        mesh=mesh,
        in_specs=(
            rows,
            rows,
            rows,
            rows,
            P("expert", "dp", None),
            P("expert", "dp", None),
            P("expert", None, "dp"),
            P(),
            rows,
        ),
        out_specs=(
            rows,
            rows,
            P("expert", "dp", None),
            P("expert", "dp", None),
            P("expert", None, "dp"),
            P("dp", "expert"),
        ),
        check_vma=False,
    )
```

```python
import math

import jax
import jax.numpy as jnp
from jax import lax
from jax.sharding import PartitionSpec as P

MOST = 10
TILE = 16


def routing_plan(picked, asked_rows, hot_list, expert_count):
    rows = picked.shape[0]
    place = jnp.arange(rows, dtype=jnp.int32)
    earlier = (picked[:, None] == picked[None, :]) & (place[None, :] < place[:, None])
    order_rank = jnp.sum(earlier.astype(jnp.int32), axis=1)
    columns = jnp.arange(expert_count, dtype=jnp.int32)
    onehot = (picked[:, None] == columns[None, :]).astype(jnp.int32)
    named_count = jnp.sum(onehot, axis=0)
    hot_match = (hot_list[:, None] == columns[None, :]).astype(jnp.int32)
    wanted = jnp.sum(hot_match * asked_rows[:, None], axis=0)
    used_rows = jnp.minimum(wanted, named_count)
    return order_rank, named_count, used_rows


def ring(value, steps):
    count = lax.axis_size("dp")
    return lax.ppermute(value, "dp", [(i, (i + steps) % count) for i in range(count)])


def quarter_starts(group, groups, width):
    return [lax.rem(group + k, groups) * width for k in range(groups)]


def to_quarters(value, group, groups, extra=None):
    rows, width = value.shape[0], value.shape[1] // groups
    parts = [
        lax.dynamic_slice(value, (0, start), (rows, width))
        for start in quarter_starts(group, groups, width)
    ]
    if extra is not None:
        parts = [jnp.concatenate([part, extra], axis=0) for part in parts]
    return [parts[0]] + [ring(parts[k], k) for k in range(1, groups)]


def from_quarters(parts, group, groups):
    rows, width = parts[0].shape
    whole = jnp.zeros((rows, groups * width), parts[0].dtype)
    for part, start in zip(parts, quarter_starts(group, groups, width)):
        whole = lax.dynamic_update_slice(whole, part, (0, start))
    return whole


def nil(earlier):
    return earlier[(0,) * earlier.ndim].astype(jnp.float32) * 0.0


def over_experts(value):
    groups, servers = lax.axis_size("dp"), lax.axis_size("expert")
    turn = servers // groups
    order = [[j * servers + (turn * j + b) % servers for b in range(servers)] for j in range(groups)]
    return lax.all_to_all(value, ("dp", "expert"), 0, 0, axis_index_groups=order, tiled=True)


def reduce_chunks(halves_of):
    f32, bf16 = jnp.float32, jnp.bfloat16
    far_first, far_second = (half.astype(bf16) for half in halves_of(2))
    up, down = ring(far_first, 1), ring(far_second, -1)
    up_first, up_second = halves_of(1)
    down_first, down_second = halves_of(3)
    up_first = (up_first + (up.astype(f32) + nil(down))).astype(bf16)
    down_second = (down_second + (down.astype(f32) + nil(up))).astype(bf16)
    first, second = halves_of(0)
    first = first + ring(down_first.astype(bf16), -1).astype(f32)
    second = second + ring(up_second.astype(bf16), 1).astype(f32)
    first = first + ring(up_first, 1).astype(f32)
    second = second + ring(down_second, -1).astype(f32)
    return jnp.concatenate([first, second], axis=0), far_first


def gather_chunks(own, zero):
    half = own.shape[0] // 2
    below, above = ring(own, 1), ring(own, -1)
    far = ring(below[:half] + zero, 1), ring(above[half:] + zero, -1)
    far = jnp.concatenate(far, axis=0)
    return own, above, far, below


def shards(tokens, cotangent, gates, expert_ids, w_gate, w_up, w_down, hot_experts, copy_counts):
    model_width = tokens.shape[1]
    tok_dev, top_count = expert_ids.shape
    row_count = tok_dev * top_count
    groups = lax.axis_size("dp")
    servers = lax.axis_size("expert")
    group = lax.axis_index("dp")
    turn = servers // groups
    grad_scale = 1.0 / math.sqrt(row_count * groups)
    gate_scale = 1.0 / math.sqrt(model_width)
    per_pair = groups * MOST
    slots = servers * per_pair
    own_slots = slots // groups
    f32, bf16 = jnp.float32, jnp.bfloat16

    chosen = expert_ids.reshape(row_count)
    order_rank, named_count, used_rows = routing_plan(chosen, copy_counts[0], hot_experts, servers)
    width = model_width // groups
    plan = jnp.stack([chosen.astype(bf16), order_rank.astype(bf16), gates.reshape(row_count)])
    plan = jnp.pad(plan, ((0, TILE - 3), (0, width - row_count)))
    tok_parts = to_quarters(tokens, group, groups, plan)
    tok_q = jnp.concatenate([part[:tok_dev] for part in tok_parts], axis=0)
    cot_q = jnp.concatenate(to_quarters(cotangent, group, groups), axis=0)

    plan = jnp.stack([part[tok_dev:tok_dev + 3, :row_count] for part in tok_parts]).astype(f32)
    source_group = lax.rem(group + groups - jnp.arange(groups, dtype=jnp.int32), groups)[:, None]
    slot_of = (plan[:, 0] * per_pair + plan[:, 1]).astype(jnp.int32) + source_group * MOST
    slot_of = slot_of.reshape(groups * tok_dev, top_count) - group * (turn * per_pair)
    slot_of = jnp.where(slot_of < 0, slot_of + slots, slot_of)
    gate_of = plan[:, 2].reshape(groups * tok_dev, top_count)
    slot_ids = jnp.arange(slots, dtype=jnp.int32)[:, None]
    hits = [slot_ids == slot_of[None, :, k] for k in range(top_count)]
    dispatch = hits[0]
    for hit in hits[1:]:
        dispatch = dispatch | hit
    dispatch = dispatch.astype(bf16)
    slot_gate = sum(
        jnp.sum(jnp.where(hit, gate_of[None, :, k], 0.0), axis=1) for k, hit in enumerate(hits)
    )
    served = (named_count - used_rows + jnp.roll(used_rows, servers // 2)).astype(f32)
    served = jnp.roll(served, -turn * group)
    small = jnp.concatenate([slot_gate.reshape(servers, per_pair), served[:, None]], axis=1)
    small = jnp.pad(small.astype(bf16)[:, None, :], ((0, 0), (0, 7), (0, width - per_pair - 1)))

    def rows_of(quarter, zero):
        rows = jnp.dot(dispatch, quarter, preferred_element_type=f32) + zero
        return rows.astype(bf16).reshape(servers, per_pair, width)

    def halves(value, k):
        middle = k * own_slots + own_slots // 2
        return value[k * own_slots:middle], value[middle:(k + 1) * own_slots]

    w_both = jnp.concatenate([w_gate[0], w_up[0]], axis=1)
    hidden_width = w_gate.shape[2]
    own_down = w_down[0]
    across = (((1,), (1,)), ((), ()))

    rows_in = over_experts(rows_of(tok_q, 0.0)).reshape(slots, width)
    pre, far = reduce_chunks(
        lambda k: [
            jnp.dot(half, w_both, preferred_element_type=f32) for half in halves(rows_in, k)
        ]
    )
    got = over_experts(jnp.concatenate([rows_of(cot_q, nil(far)), small], axis=1))
    rows_cot = got[:, :per_pair].reshape(slots, width)
    load_here = jnp.sum(got[:, per_pair, per_pair].astype(f32)) / row_count
    row_gate = got[:turn, per_pair, :per_pair].astype(f32).reshape(own_slots, 1)
    zero = nil(pre)
    back, _ = reduce_chunks(
        lambda k: [
            lax.dot_general(half, own_down, across, preferred_element_type=f32) + zero
            for half in halves(rows_cot, k)
        ]
    )

    gate_pre, up_pre = pre[:, :hidden_width], pre[:, hidden_width:]
    sigmoid = jax.nn.sigmoid(gate_pre)
    active = gate_pre * sigmoid
    hidden = active * up_pre
    d_gate_rows = jnp.sum(hidden * back, axis=1) * gate_scale
    d_hidden = row_gate * back
    d_gate_pre = d_hidden * up_pre * sigmoid * (1.0 + gate_pre * (1.0 - sigmoid))
    d_up_pre = d_hidden * active
    d_both = jnp.concatenate([d_gate_pre.astype(bf16), d_up_pre.astype(bf16)], axis=1)
    gated = hidden * row_gate

    own_gate = d_gate_rows.reshape(turn, per_pair)
    own_gate = over_experts(jnp.pad(own_gate, ((0, servers - turn), (0, 0))))
    d_parts = gather_chunks(d_both, nil(own_gate).astype(bf16))
    d_rows = [
        lax.dot_general(part, w_both, across, preferred_element_type=f32).astype(bf16)
        for part in d_parts
    ]
    back_rows = over_experts(jnp.concatenate(d_rows, axis=0).reshape(servers, per_pair, width))
    back_rows = back_rows.reshape(slots, width)
    d_both = jnp.concatenate(d_parts, axis=0)
    gated = (gated + nil(d_rows[2])).astype(bf16)
    gated = jnp.concatenate([gated] + [ring(gated, -k) for k in range(1, groups)], axis=0)

    outer = (((0,), (0,)), ((), ()))
    grad_both = [
        (lax.dot_general(rows_in, part, outer, preferred_element_type=f32) * grad_scale).astype(bf16)
        for part in (d_both[:, :hidden_width], d_both[:, hidden_width:])
    ]
    grad_down = lax.dot_general(gated, rows_cot, outer, preferred_element_type=f32)
    grad_down = (grad_down * grad_scale).astype(bf16)

    zero = nil(grad_both[0]) + nil(grad_both[1]) + nil(grad_down)
    d_tok_q = lax.dot_general(dispatch, back_rows, outer, preferred_element_type=f32) + zero
    d_tok_q = d_tok_q.astype(bf16).reshape(groups, tok_dev, width)
    by_group = jnp.roll(own_gate, turn * group, axis=0)
    by_group = by_group.reshape(servers, groups, MOST).transpose(1, 0, 2).reshape(groups, -1)
    by_group = by_group[source_group[:, 0]].astype(bf16)[:, None, :]
    by_group = jnp.pad(by_group, ((0, 0), (0, TILE - 1), (0, width - servers * MOST)))
    parts = jnp.concatenate([d_tok_q, by_group], axis=1)
    parts = [parts[0]] + [ring(parts[k], -k) for k in range(1, groups)]
    d_tokens = from_quarters([part[:tok_dev] for part in parts], group, groups)

    mine = sum(part[tok_dev:tok_dev + 1, :servers * MOST].astype(f32) for part in parts)
    spot = chosen * MOST + order_rank
    match = spot[:, None] == jnp.arange(servers * MOST, dtype=jnp.int32)[None, :]
    d_gates = jnp.sum(jnp.where(match, mine, 0.0), axis=1).astype(bf16).reshape(tok_dev, top_count)
    return (
        d_tokens,
        d_gates,
        grad_both[0][None],
        grad_both[1][None],
        grad_down[None],
        load_here.reshape(1, 1),
    )


def solution(mesh):
    rows = P(("dp", "expert"), None)
    return jax.shard_map(
        shards,
        mesh=mesh,
        in_specs=(
            rows,
            rows,
            rows,
            rows,
            P("expert", "dp", None),
            P("expert", "dp", None),
            P("expert", None, "dp"),
            P(),
            rows,
        ),
        out_specs=(
            rows,
            rows,
            P("expert", "dp", None),
            P("expert", "dp", None),
            P("expert", None, "dp"),
            P("dp", "expert"),
        ),
        check_vma=False,
    )
```

```python
import math

import jax
import jax.numpy as jnp
from jax import lax
from jax.sharding import PartitionSpec as P

MOST = 10
TILE = 16


def routing_plan(picked, asked_rows, hot_list, expert_count):
    rows = picked.shape[0]
    place = jnp.arange(rows, dtype=jnp.int32)
    earlier = (picked[:, None] == picked[None, :]) & (place[None, :] < place[:, None])
    order_rank = jnp.sum(earlier.astype(jnp.int32), axis=1)
    columns = jnp.arange(expert_count, dtype=jnp.int32)
    onehot = (picked[:, None] == columns[None, :]).astype(jnp.int32)
    named_count = jnp.sum(onehot, axis=0)
    hot_match = (hot_list[:, None] == columns[None, :]).astype(jnp.int32)
    wanted = jnp.sum(hot_match * asked_rows[:, None], axis=0)
    used_rows = jnp.minimum(wanted, named_count)
    return order_rank, named_count, used_rows


def ring(value, steps):
    count = lax.axis_size("dp")
    return lax.ppermute(value, "dp", [(i, (i + steps) % count) for i in range(count)])


def quarter_starts(group, groups, width):
    return [lax.rem(group + k, groups) * width for k in range(groups)]


def to_quarters(value, group, groups, extra=None):
    rows, width = value.shape[0], value.shape[1] // groups
    parts = [
        lax.dynamic_slice(value, (0, start), (rows, width))
        for start in quarter_starts(group, groups, width)
    ]
    if extra is not None:
        parts = [jnp.concatenate([part, extra], axis=0) for part in parts]
    return [parts[0]] + [ring(parts[k], k) for k in range(1, groups)]


def from_quarters(parts, group, groups):
    whole = []
    for quarter in range(groups):
        spot = lax.rem(quarter + groups - group, groups)
        piece = parts[0]
        for k in range(1, groups):
            piece = jnp.where(spot == k, parts[k], piece)
        whole.append(piece)
    return jnp.concatenate(whole, axis=1)


def nil(earlier):
    return earlier[(0,) * earlier.ndim].astype(jnp.float32) * 0.0


def over_experts(value):
    groups, servers = lax.axis_size("dp"), lax.axis_size("expert")
    turn = servers // groups
    order = [[j * servers + (turn * j + b) % servers for b in range(servers)] for j in range(groups)]
    return lax.all_to_all(value, ("dp", "expert"), 0, 0, axis_index_groups=order, tiled=True)


def reduce_chunks(halves_of):
    f32, bf16 = jnp.float32, jnp.bfloat16
    far_first, far_second = (half.astype(bf16) for half in halves_of(2))
    up, down = ring(far_first, 1), ring(far_second, -1)
    up_first, up_second = halves_of(1)
    down_first, down_second = halves_of(3)
    up, down = up.astype(f32), down.astype(f32)
    up_first = (up_first + (up + down * 0.0)).astype(bf16)
    down_second = (down_second + (down + up * 0.0)).astype(bf16)
    first, second = halves_of(0)
    first = first + ring(down_first.astype(bf16), -1).astype(f32)
    second = second + ring(up_second.astype(bf16), 1).astype(f32)
    first = first + ring(up_first, 1).astype(f32)
    second = second + ring(down_second, -1).astype(f32)
    return jnp.concatenate([first, second], axis=0), far_first


def gather_chunks(own, zero):
    half = own.shape[0] // 2
    below, above = ring(own, 1), ring(own, -1)
    far = ring(below[:half] + zero, 1), ring(above[half:] + zero, -1)
    far = jnp.concatenate(far, axis=0)
    return own, above, far, below


def shards(tokens, cotangent, gates, expert_ids, w_gate, w_up, w_down, hot_experts, copy_counts):
    model_width = tokens.shape[1]
    tok_dev, top_count = expert_ids.shape
    row_count = tok_dev * top_count
    groups = lax.axis_size("dp")
    servers = lax.axis_size("expert")
    group = lax.axis_index("dp")
    turn = servers // groups
    grad_scale = 1.0 / math.sqrt(row_count * groups)
    gate_scale = 1.0 / math.sqrt(model_width)
    per_pair = groups * MOST
    slots = servers * per_pair
    own_slots = slots // groups
    f32, bf16 = jnp.float32, jnp.bfloat16

    chosen = expert_ids.reshape(row_count)
    order_rank, named_count, used_rows = routing_plan(chosen, copy_counts[0], hot_experts, servers)
    width = model_width // groups
    plan = jnp.stack([chosen.astype(bf16), order_rank.astype(bf16), gates.reshape(row_count)])
    plan = jnp.pad(plan, ((0, TILE - 3), (0, width - row_count)))
    tok_parts = to_quarters(tokens, group, groups, plan)
    tok_q = jnp.concatenate([part[:tok_dev] for part in tok_parts], axis=0)
    cot_q = jnp.concatenate(to_quarters(cotangent, group, groups), axis=0)

    plan = jnp.stack([part[tok_dev:tok_dev + 3, :row_count] for part in tok_parts]).astype(f32)
    source_group = lax.rem(group + groups - jnp.arange(groups, dtype=jnp.int32), groups)[:, None]
    slot_of = (plan[:, 0] * per_pair + plan[:, 1]).astype(jnp.int32) + source_group * MOST
    slot_of = slot_of.reshape(groups * tok_dev, top_count) - group * (turn * per_pair)
    slot_of = jnp.where(slot_of < 0, slot_of + slots, slot_of)
    gate_of = plan[:, 2].reshape(groups * tok_dev, top_count)
    slot_ids = jnp.arange(slots, dtype=jnp.int32)[:, None]
    hits = [slot_ids == slot_of[None, :, k] for k in range(top_count)]
    dispatch = hits[0]
    for hit in hits[1:]:
        dispatch = dispatch | hit
    dispatch = dispatch.astype(bf16)
    slot_gate = sum(
        jnp.sum(jnp.where(hit, gate_of[None, :, k], 0.0), axis=1) for k, hit in enumerate(hits)
    )
    served = (named_count - used_rows + jnp.roll(used_rows, servers // 2)).astype(f32)
    served = jnp.roll(served, -turn * group)
    small = jnp.concatenate([slot_gate.reshape(servers, per_pair), served[:, None]], axis=1)
    small = jnp.pad(small.astype(bf16)[:, None, :], ((0, 0), (0, 7), (0, width - per_pair - 1)))

    def rows_of(quarter, zero):
        rows = jnp.dot(dispatch, quarter, preferred_element_type=f32) + zero
        return rows.astype(bf16).reshape(servers, per_pair, width)

    def halves(value, k):
        middle = k * own_slots + own_slots // 2
        return value[k * own_slots:middle], value[middle:(k + 1) * own_slots]

    w_both = jnp.concatenate([w_gate[0], w_up[0]], axis=1)
    hidden_width = w_gate.shape[2]
    own_down = w_down[0]
    across = (((1,), (1,)), ((), ()))

    rows_in = over_experts(rows_of(tok_q, 0.0)).reshape(slots, width)
    pre, far = reduce_chunks(
        lambda k: [
            jnp.dot(half, w_both, preferred_element_type=f32) for half in halves(rows_in, k)
        ]
    )
    got = over_experts(jnp.concatenate([rows_of(cot_q, nil(far)), small], axis=1))
    rows_cot = got[:, :per_pair].reshape(slots, width)
    row_gate = got[:turn, per_pair, :per_pair].astype(f32).reshape(own_slots, 1)
    zero = pre[:own_slots // 2, :hidden_width] * 0.0
    back, _ = reduce_chunks(
        lambda k: [
            lax.dot_general(half, own_down, across, preferred_element_type=f32) + zero
            for half in halves(rows_cot, k)
        ]
    )

    gate_pre, up_pre = pre[:, :hidden_width], pre[:, hidden_width:]
    sigmoid = jax.nn.sigmoid(gate_pre)
    active = gate_pre * sigmoid
    hidden = active * up_pre
    d_gate_rows = jnp.sum(hidden * back, axis=1) * gate_scale
    d_hidden = row_gate * back
    d_gate_pre = d_hidden * up_pre * sigmoid * (1.0 + gate_pre * (1.0 - sigmoid))
    d_up_pre = d_hidden * active
    d_both = jnp.concatenate([d_gate_pre.astype(bf16), d_up_pre.astype(bf16)], axis=1)
    gated = hidden * row_gate

    own_gate = d_gate_rows.reshape(turn, per_pair)
    own_gate = over_experts(jnp.pad(own_gate, ((0, servers - turn), (0, 0))))
    d_parts = gather_chunks(d_both, nil(own_gate).astype(bf16))
    d_rows = [
        lax.dot_general(part, w_both, across, preferred_element_type=f32).astype(bf16)
        for part in d_parts
    ]
    send_rows = jnp.concatenate(d_rows, axis=0)
    back_rows = over_experts(send_rows.reshape(servers, per_pair, width)).reshape(slots, width)
    zero = nil(d_rows[2])
    load_here = (jnp.sum(got[:, per_pair, per_pair].astype(f32)) + zero) / row_count
    d_both = jnp.concatenate(d_parts, axis=0)
    gated = (gated + zero).astype(bf16)
    gated = [gated] + [ring(gated, -k) for k in range(1, groups)]

    outer = (((0,), (0,)), ((), ()))
    grad_both = [
        (lax.dot_general(rows_in, part, outer, preferred_element_type=f32) * grad_scale).astype(bf16)
        for part in (d_both[:, :hidden_width], d_both[:, hidden_width:])
    ]
    zero = nil(grad_both[0]) + nil(grad_both[1])
    d_tok_q = lax.dot_general(dispatch, back_rows, outer, preferred_element_type=f32) + zero
    d_tok_q = d_tok_q.astype(bf16).reshape(groups, tok_dev, width)
    gated = jnp.concatenate(gated, axis=0) + nil(d_tok_q).astype(bf16)
    gated = jnp.pad(gated.reshape(servers, per_pair, hidden_width), ((0, 0), (0, 8), (0, 0)))
    gated, got = gated.reshape(-1, hidden_width), got.reshape(-1, width)
    grad_down = lax.dot_general(gated, got, outer, preferred_element_type=f32)
    grad_down = (grad_down * grad_scale).astype(bf16)

    by_group = jnp.roll(own_gate, turn * group, axis=0)
    by_group = by_group.reshape(servers, groups, MOST).transpose(1, 0, 2).reshape(groups, -1)
    by_group = by_group[source_group[:, 0]].astype(bf16)[:, None, :]
    by_group = jnp.pad(by_group, ((0, 0), (0, TILE - 1), (0, width - servers * MOST)))
    parts = jnp.concatenate([d_tok_q, by_group], axis=1)
    parts = [parts[0]] + [ring(parts[k], -k) for k in range(1, groups)]
    d_tokens = from_quarters([part[:tok_dev] for part in parts], group, groups)

    mine = sum(part[tok_dev:tok_dev + 1, :servers * MOST].astype(f32) for part in parts)
    mine = mine + nil(grad_down)
    spot = chosen * MOST + order_rank
    match = spot[:, None] == jnp.arange(servers * MOST, dtype=jnp.int32)[None, :]
    d_gates = jnp.sum(jnp.where(match, mine, 0.0), axis=1).astype(bf16).reshape(tok_dev, top_count)
    return (
        d_tokens,
        d_gates,
        grad_both[0][None],
        grad_both[1][None],
        grad_down[None],
        load_here.reshape(1, 1),
    )


def solution(mesh):
    rows = P(("dp", "expert"), None)
    return jax.shard_map(
        shards,
        mesh=mesh,
        in_specs=(
            rows,
            rows,
            rows,
            rows,
            P("expert", "dp", None),
            P("expert", "dp", None),
            P("expert", None, "dp"),
            P(),
            rows,
        ),
        out_specs=(
            rows,
            rows,
            P("expert", "dp", None),
            P("expert", "dp", None),
            P("expert", None, "dp"),
            P("dp", "expert"),
        ),
        check_vma=False,
    )
```

```python
import math

import jax
import jax.numpy as jnp
from jax import lax
from jax.sharding import PartitionSpec as P

MOST = 10
TILE = 16


def routing_plan(picked, asked_rows, hot_list, expert_count):
    rows = picked.shape[0]
    place = jnp.arange(rows, dtype=jnp.int32)
    earlier = (picked[:, None] == picked[None, :]) & (place[None, :] < place[:, None])
    order_rank = jnp.sum(earlier.astype(jnp.int32), axis=1)
    columns = jnp.arange(expert_count, dtype=jnp.int32)
    onehot = (picked[:, None] == columns[None, :]).astype(jnp.int32)
    named_count = jnp.sum(onehot, axis=0)
    hot_match = (hot_list[:, None] == columns[None, :]).astype(jnp.int32)
    wanted = jnp.sum(hot_match * asked_rows[:, None], axis=0)
    used_rows = jnp.minimum(wanted, named_count)
    return order_rank, named_count, used_rows


def ring(value, steps):
    count = lax.axis_size("dp")
    return lax.ppermute(value, "dp", [(i, (i + steps) % count) for i in range(count)])


def quarter_starts(group, groups, width):
    return [lax.rem(group + k, groups) * width for k in range(groups)]


def to_quarters(value, group, groups, extra=None):
    rows, width = value.shape[0], value.shape[1] // groups
    parts = [
        lax.dynamic_slice(value, (0, start), (rows, width))
        for start in quarter_starts(group, groups, width)
    ]
    if extra is not None:
        parts = [jnp.concatenate([part, extra], axis=0) for part in parts]
    return [parts[0]] + [ring(parts[k], k) for k in range(1, groups)]


def from_quarters(parts, group, groups):
    whole = []
    for quarter in range(groups):
        spot = lax.rem(quarter + groups - group, groups)
        piece = parts[0]
        for k in range(1, groups):
            piece = jnp.where(spot == k, parts[k], piece)
        whole.append(piece)
    return jnp.concatenate(whole, axis=1)


def nil(earlier):
    return earlier[(0,) * earlier.ndim].astype(jnp.float32) * 0.0


def over_experts(value):
    groups, servers = lax.axis_size("dp"), lax.axis_size("expert")
    turn = servers // groups
    order = [[j * servers + (turn * j + b) % servers for b in range(servers)] for j in range(groups)]
    return lax.all_to_all(value, ("dp", "expert"), 0, 0, axis_index_groups=order, tiled=True)


def reduce_chunks(far, halves_of, hold):
    f32, bf16 = jnp.float32, jnp.bfloat16
    up, down = ring(far[0], 1).astype(f32), ring(far[1], -1).astype(f32)
    up_first, up_second = halves_of(1)
    down_first, down_second = halves_of(3)
    down_first, up_second = (down_first + hold).astype(bf16), (up_second + hold).astype(bf16)
    up_first = (up_first + (up + down * 0.0)).astype(bf16)
    down_second = (down_second + (down + up * 0.0)).astype(bf16)
    first, second = halves_of(0)
    first = first + ring(down_first, -1).astype(f32)
    second = second + ring(up_second, 1).astype(f32)
    first = first + ring(up_first, 1).astype(f32)
    second = second + ring(down_second, -1).astype(f32)
    return jnp.concatenate([first, second], axis=0)


def gather_chunks(own, zero):
    half = own.shape[0] // 2
    below, above = ring(own, 1), ring(own, -1)
    far = ring(below[:half] + zero, 1), ring(above[half:] + zero, -1)
    far = jnp.concatenate(far, axis=0)
    return own, above, far, below


def shards(tokens, cotangent, gates, expert_ids, w_gate, w_up, w_down, hot_experts, copy_counts):
    model_width = tokens.shape[1]
    tok_dev, top_count = expert_ids.shape
    row_count = tok_dev * top_count
    groups = lax.axis_size("dp")
    servers = lax.axis_size("expert")
    group = lax.axis_index("dp")
    turn = servers // groups
    grad_scale = 1.0 / math.sqrt(row_count * groups)
    gate_scale = 1.0 / math.sqrt(model_width)
    per_pair = groups * MOST
    slots = servers * per_pair
    own_slots = slots // groups
    f32, bf16 = jnp.float32, jnp.bfloat16

    chosen = expert_ids.reshape(row_count)
    order_rank, named_count, used_rows = routing_plan(chosen, copy_counts[0], hot_experts, servers)
    width = model_width // groups
    plan = jnp.stack([chosen.astype(bf16), order_rank.astype(bf16), gates.reshape(row_count)])
    plan = jnp.pad(plan, ((0, TILE - 3), (0, width - row_count)))
    tok_parts = to_quarters(tokens, group, groups, plan)
    tok_q = jnp.concatenate([part[:tok_dev] for part in tok_parts], axis=0)
    cot_q = jnp.concatenate(to_quarters(cotangent, group, groups), axis=0)

    plan = jnp.stack([part[tok_dev:tok_dev + 3, :row_count] for part in tok_parts]).astype(f32)
    source_group = lax.rem(group + groups - jnp.arange(groups, dtype=jnp.int32), groups)[:, None]
    slot_of = (plan[:, 0] * per_pair + plan[:, 1]).astype(jnp.int32) + source_group * MOST
    slot_of = slot_of.reshape(groups * tok_dev, top_count) - group * (turn * per_pair)
    slot_of = jnp.where(slot_of < 0, slot_of + slots, slot_of)
    gate_of = plan[:, 2].reshape(groups * tok_dev, top_count)
    slot_ids = jnp.arange(slots, dtype=jnp.int32)[:, None]
    hits = [slot_ids == slot_of[None, :, k] for k in range(top_count)]
    dispatch = hits[0]
    for hit in hits[1:]:
        dispatch = dispatch | hit
    dispatch = dispatch.astype(bf16)
    slot_gate = sum(
        jnp.sum(jnp.where(hit, gate_of[None, :, k], 0.0), axis=1) for k, hit in enumerate(hits)
    )
    served = (named_count - used_rows + jnp.roll(used_rows, servers // 2)).astype(f32)
    served = jnp.roll(served, -turn * group)
    small = jnp.concatenate([slot_gate.reshape(servers, per_pair), served[:, None]], axis=1)
    small = jnp.pad(small.astype(bf16)[:, None, :], ((0, 0), (0, 7), (0, width - per_pair - 1)))

    def rows_of(quarter):
        rows = jnp.dot(dispatch, quarter, preferred_element_type=f32)
        return rows.astype(bf16).reshape(servers, per_pair, width)

    def halves(value, k):
        middle = k * own_slots + own_slots // 2
        return value[k * own_slots:middle], value[middle:(k + 1) * own_slots]

    w_both = jnp.concatenate([w_gate[0], w_up[0]], axis=1)
    hidden_width = w_gate.shape[2]
    own_down = w_down[0]
    across = (((1,), (1,)), ((), ()))

    rows_in = over_experts(rows_of(tok_q)).reshape(slots, width)
    def pre_halves(k):
        return [jnp.dot(half, w_both, preferred_element_type=f32) for half in halves(rows_in, k)]

    far = [half.astype(bf16) for half in pre_halves(2)]
    small = small + (far[0][:8, :width] * 0.0 + far[1][:8, :width] * 0.0)
    send_cot = jnp.concatenate([rows_of(cot_q), small], axis=1)
    got = over_experts(send_cot)
    pre = reduce_chunks(far, pre_halves, jnp.max(send_cot[:, per_pair - 8:, :128]).astype(f32) * 0.0)
    rows_cot = got[:, :per_pair].reshape(slots, width)
    row_gate = got[:turn, per_pair, :per_pair].astype(f32).reshape(own_slots, 1)
    zero = pre[:own_slots // 2, :hidden_width] * 0.0

    def back_halves(k):
        return [
            lax.dot_general(half, own_down, across, preferred_element_type=f32) + zero
            for half in halves(rows_cot, k)
        ]

    back = reduce_chunks([half.astype(bf16) for half in back_halves(2)], back_halves, 0.0)

    gate_pre, up_pre = pre[:, :hidden_width], pre[:, hidden_width:]
    sigmoid = jax.nn.sigmoid(gate_pre)
    active = gate_pre * sigmoid
    hidden = active * up_pre
    d_gate_rows = jnp.sum(hidden * back, axis=1) * gate_scale
    d_hidden = row_gate * back
    d_gate_pre = d_hidden * up_pre * sigmoid * (1.0 + gate_pre * (1.0 - sigmoid))
    d_up_pre = d_hidden * active
    d_both = jnp.concatenate([d_gate_pre.astype(bf16), d_up_pre.astype(bf16)], axis=1)
    gated = hidden * row_gate

    own_gate = d_gate_rows.reshape(turn, per_pair)
    own_gate = over_experts(jnp.pad(own_gate, ((0, servers - turn), (0, 0))))
    d_parts = gather_chunks(d_both, nil(own_gate).astype(bf16))
    d_rows = [
        lax.dot_general(part, w_both, across, preferred_element_type=f32).astype(bf16)
        for part in d_parts
    ]
    send_rows = jnp.concatenate(d_rows, axis=0)
    back_rows = over_experts(send_rows.reshape(servers, per_pair, width)).reshape(slots, width)
    zero = nil(d_rows[2])
    load_here = (jnp.sum(got[:, per_pair, per_pair].astype(f32)) + zero) / row_count
    d_both = jnp.concatenate(d_parts, axis=0)
    gated = (gated + zero).astype(bf16)
    gated = [gated] + [ring(gated, -k) for k in range(1, groups)]

    outer = (((0,), (0,)), ((), ()))
    grad_both = [
        (lax.dot_general(rows_in, part, outer, preferred_element_type=f32) * grad_scale).astype(bf16)
        for part in (d_both[:, :hidden_width], d_both[:, hidden_width:])
    ]
    zero = nil(grad_both[0]) + nil(grad_both[1])
    d_tok_q = lax.dot_general(dispatch, back_rows, outer, preferred_element_type=f32) + zero
    d_tok_q = d_tok_q.astype(bf16).reshape(groups, tok_dev, width)
    gated = jnp.concatenate(gated, axis=0) + nil(d_tok_q).astype(bf16)
    gated = jnp.pad(gated.reshape(servers, per_pair, hidden_width), ((0, 0), (0, 8), (0, 0)))
    gated, got = gated.reshape(-1, hidden_width), got.reshape(-1, width)
    grad_down = lax.dot_general(gated, got, outer, preferred_element_type=f32)
    grad_down = (grad_down * grad_scale).astype(bf16)

    by_group = jnp.roll(own_gate, turn * group, axis=0)
    by_group = by_group.reshape(servers, groups, MOST).transpose(1, 0, 2).reshape(groups, -1)
    by_group = by_group[source_group[:, 0]].astype(bf16)[:, None, :]
    by_group = jnp.pad(by_group, ((0, 0), (0, TILE - 1), (0, width - servers * MOST)))
    parts = jnp.concatenate([d_tok_q, by_group], axis=1)
    parts = [parts[0]] + [ring(parts[k], -k) for k in range(1, groups)]
    d_tokens = from_quarters([part[:tok_dev] for part in parts], group, groups)

    mine = sum(part[tok_dev:tok_dev + 1, :servers * MOST].astype(f32) for part in parts)
    mine = mine + nil(grad_down)
    spot = chosen * MOST + order_rank
    match = spot[:, None] == jnp.arange(servers * MOST, dtype=jnp.int32)[None, :]
    d_gates = jnp.sum(jnp.where(match, mine, 0.0), axis=1).astype(bf16).reshape(tok_dev, top_count)
    return (
        d_tokens,
        d_gates,
        grad_both[0][None],
        grad_both[1][None],
        grad_down[None],
        load_here.reshape(1, 1),
    )


def solution(mesh):
    rows = P(("dp", "expert"), None)
    return jax.shard_map(
        shards,
        mesh=mesh,
        in_specs=(
            rows,
            rows,
            rows,
            rows,
            P("expert", "dp", None),
            P("expert", "dp", None),
            P("expert", None, "dp"),
            P(),
            rows,
        ),
        out_specs=(
            rows,
            rows,
            P("expert", "dp", None),
            P("expert", "dp", None),
            P("expert", None, "dp"),
            P("dp", "expert"),
        ),
        check_vma=False,
    )
```

```python
import math

import jax
import jax.numpy as jnp
from jax import lax
from jax.sharding import PartitionSpec as P

MOST = 10
TILE = 16


def routing_plan(picked, asked_rows, hot_list, expert_count):
    rows = picked.shape[0]
    place = jnp.arange(rows, dtype=jnp.int32)
    earlier = (picked[:, None] == picked[None, :]) & (place[None, :] < place[:, None])
    order_rank = jnp.sum(earlier.astype(jnp.int32), axis=1)
    columns = jnp.arange(expert_count, dtype=jnp.int32)
    onehot = (picked[:, None] == columns[None, :]).astype(jnp.int32)
    named_count = jnp.sum(onehot, axis=0)
    hot_match = (hot_list[:, None] == columns[None, :]).astype(jnp.int32)
    wanted = jnp.sum(hot_match * asked_rows[:, None], axis=0)
    used_rows = jnp.minimum(wanted, named_count)
    return order_rank, named_count, used_rows


def ring(value, steps):
    count = lax.axis_size("dp")
    return lax.ppermute(value, "dp", [(i, (i + steps) % count) for i in range(count)])


def quarter_starts(group, groups, width):
    return [lax.rem(group + k, groups) * width for k in range(groups)]


def to_quarters(value, group, groups, extra=None):
    rows, width = value.shape[0], value.shape[1] // groups
    parts = [
        lax.dynamic_slice(value, (0, start), (rows, width))
        for start in quarter_starts(group, groups, width)
    ]
    if extra is not None:
        parts = [jnp.concatenate([part, extra], axis=0) for part in parts]
    return [parts[0]] + [ring(parts[k], k) for k in range(1, groups)]


def from_quarters(parts, group, groups):
    whole = []
    for quarter in range(groups):
        spot = lax.rem(quarter + groups - group, groups)
        piece = parts[0]
        for k in range(1, groups):
            piece = jnp.where(spot == k, parts[k], piece)
        whole.append(piece)
    return jnp.concatenate(whole, axis=1)


def nil(earlier):
    return earlier[(0,) * earlier.ndim].astype(jnp.float32) * 0.0


def over_experts(value):
    groups, servers = lax.axis_size("dp"), lax.axis_size("expert")
    turn = servers // groups
    order = [[j * servers + (turn * j + b) % servers for b in range(servers)] for j in range(groups)]
    return lax.all_to_all(value, ("dp", "expert"), 0, 0, axis_index_groups=order, tiled=True)


def reduce_chunks(far, halves_of, hold):
    f32, bf16 = jnp.float32, jnp.bfloat16
    up, down = ring(far[0], 1).astype(f32), ring(far[1], -1).astype(f32)
    up_first, up_second = halves_of(1)
    down_first, down_second = halves_of(3)
    down_first, up_second = (down_first + hold).astype(bf16), (up_second + hold).astype(bf16)
    up_first = (up_first + (up + down * 0.0)).astype(bf16)
    down_second = (down_second + (down + up * 0.0)).astype(bf16)
    first, second = halves_of(0)
    first = first + ring(down_first, -1).astype(f32)
    second = second + ring(up_second, 1).astype(f32)
    first = first + ring(up_first, 1).astype(f32)
    second = second + ring(down_second, -1).astype(f32)
    return jnp.concatenate([first, second], axis=0)


def gather_chunks(own, zero):
    half = own.shape[0] // 2
    below, above = ring(own, 1), ring(own, -1)
    far = ring(below[:half] + zero, 1), ring(above[half:] + zero, -1)
    far = jnp.concatenate(far, axis=0)
    return own, above, far, below


def shards(tokens, cotangent, gates, expert_ids, w_gate, w_up, w_down, hot_experts, copy_counts):
    model_width = tokens.shape[1]
    tok_dev, top_count = expert_ids.shape
    row_count = tok_dev * top_count
    groups = lax.axis_size("dp")
    servers = lax.axis_size("expert")
    group = lax.axis_index("dp")
    turn = servers // groups
    grad_scale = 1.0 / math.sqrt(row_count * groups)
    gate_scale = 1.0 / math.sqrt(model_width)
    per_pair = groups * MOST
    slots = servers * per_pair
    own_slots = slots // groups
    f32, bf16 = jnp.float32, jnp.bfloat16

    chosen = expert_ids.reshape(row_count)
    order_rank, named_count, used_rows = routing_plan(chosen, copy_counts[0], hot_experts, servers)
    width = model_width // groups
    plan = jnp.stack([chosen.astype(bf16), order_rank.astype(bf16), gates.reshape(row_count)])
    plan = jnp.pad(plan, ((0, TILE - 3), (0, width - row_count)))
    tok_parts = to_quarters(tokens, group, groups, plan)
    tok_q = jnp.concatenate([part[:tok_dev] for part in tok_parts], axis=0)
    cot_q = jnp.concatenate(to_quarters(cotangent, group, groups), axis=0)

    plan = jnp.stack([part[tok_dev:tok_dev + 3, :row_count] for part in tok_parts]).astype(f32)
    source_group = lax.rem(group + groups - jnp.arange(groups, dtype=jnp.int32), groups)[:, None]
    slot_of = (plan[:, 0] * per_pair + plan[:, 1]).astype(jnp.int32) + source_group * MOST
    slot_of = slot_of.reshape(groups * tok_dev, top_count) - group * (turn * per_pair)
    slot_of = jnp.where(slot_of < 0, slot_of + slots, slot_of)
    gate_of = plan[:, 2].reshape(groups * tok_dev, top_count)
    slot_ids = jnp.arange(slots, dtype=jnp.int32)[:, None]
    hits = [slot_ids == slot_of[None, :, k] for k in range(top_count)]
    dispatch = hits[0]
    for hit in hits[1:]:
        dispatch = dispatch | hit
    dispatch = dispatch.astype(bf16)
    slot_gate = sum(
        jnp.sum(jnp.where(hit, gate_of[None, :, k], 0.0), axis=1) for k, hit in enumerate(hits)
    )
    served = (named_count - used_rows + jnp.roll(used_rows, servers // 2)).astype(f32)
    served = jnp.roll(served, -turn * group)
    small = jnp.concatenate([slot_gate.reshape(servers, per_pair), served[:, None]], axis=1)

    def rows_of(quarter):
        rows = jnp.dot(dispatch, quarter, preferred_element_type=f32)
        return rows.astype(bf16).reshape(servers, per_pair, width)

    def halves(value, k):
        middle = k * own_slots + own_slots // 2
        return value[k * own_slots:middle], value[middle:(k + 1) * own_slots]

    w_both = jnp.concatenate([w_gate[0], w_up[0]], axis=1)
    hidden_width = w_gate.shape[2]
    own_down = w_down[0]
    across = (((1,), (1,)), ((), ()))

    rows_in = over_experts(rows_of(tok_q)).reshape(slots, width)
    def pre_halves(k):
        return [jnp.dot(half, w_both, preferred_element_type=f32) for half in halves(rows_in, k)]

    far = [half.astype(bf16) for half in pre_halves(2)]
    small = small.astype(bf16)
    small = small + (far[0][:servers, :per_pair + 1] + far[1][:servers, :per_pair + 1]) * 0.0
    small = jnp.pad(small[:, None, :], ((0, 0), (0, 7), (0, width - per_pair - 1)))
    send_cot = jnp.concatenate([rows_of(cot_q), small], axis=1)
    got = over_experts(send_cot)
    pre = reduce_chunks(far, pre_halves, jnp.max(send_cot[:, per_pair - 8:, :128]).astype(f32) * 0.0)
    rows_cot = got[:, :per_pair].reshape(slots, width)
    row_gate = got[:turn, per_pair, :per_pair].astype(f32).reshape(own_slots, 1)
    zero = pre[:own_slots // 2, :hidden_width] * 0.0

    def back_halves(k):
        return [
            lax.dot_general(half, own_down, across, preferred_element_type=f32) + zero
            for half in halves(rows_cot, k)
        ]

    back = reduce_chunks([half.astype(bf16) for half in back_halves(2)], back_halves, 0.0)

    gate_pre, up_pre = pre[:, :hidden_width], pre[:, hidden_width:]
    sigmoid = jax.nn.sigmoid(gate_pre)
    active = gate_pre * sigmoid
    hidden = active * up_pre
    d_gate_rows = jnp.sum(hidden * back, axis=1) * gate_scale
    d_hidden = row_gate * back
    d_gate_pre = d_hidden * up_pre * sigmoid * (1.0 + gate_pre * (1.0 - sigmoid))
    d_up_pre = d_hidden * active
    d_both = jnp.concatenate([d_gate_pre.astype(bf16), d_up_pre.astype(bf16)], axis=1)
    gated = hidden * row_gate

    own_gate = d_gate_rows.reshape(turn, per_pair)
    own_gate = over_experts(jnp.pad(own_gate, ((0, servers - turn), (0, 0))))
    d_parts = gather_chunks(d_both, nil(own_gate).astype(bf16))
    d_rows = [
        lax.dot_general(part, w_both, across, preferred_element_type=f32).astype(bf16)
        for part in d_parts
    ]
    send_rows = jnp.concatenate(d_rows, axis=0)
    back_rows = over_experts(send_rows.reshape(servers, per_pair, width)).reshape(slots, width)
    zero = nil(d_rows[2])
    load_here = (jnp.sum(got[:, per_pair, per_pair].astype(f32)) + zero) / row_count
    d_both = jnp.concatenate(d_parts, axis=0)
    gated = (gated + zero).astype(bf16)
    gated = [gated] + [ring(gated, -k) for k in range(1, groups)]

    outer = (((0,), (0,)), ((), ()))
    grad_both = [
        (lax.dot_general(rows_in, part, outer, preferred_element_type=f32) * grad_scale).astype(bf16)
        for part in (d_both[:, :hidden_width], d_both[:, hidden_width:])
    ]
    zero = nil(grad_both[0]) + nil(grad_both[1])
    d_tok_q = lax.dot_general(dispatch, back_rows, outer, preferred_element_type=f32) + zero
    d_tok_q = d_tok_q.astype(bf16).reshape(groups, tok_dev, width)
    gated = jnp.concatenate(gated, axis=0) + nil(d_tok_q).astype(bf16)
    gated = jnp.pad(gated.reshape(servers, per_pair, hidden_width), ((0, 0), (0, 8), (0, 0)))
    gated, got = gated.reshape(-1, hidden_width), got.reshape(-1, width)
    grad_down = lax.dot_general(gated, got, outer, preferred_element_type=f32)
    grad_down = (grad_down * grad_scale).astype(bf16)

    by_group = jnp.roll(own_gate, turn * group, axis=0)
    by_group = by_group.reshape(servers, groups, MOST).transpose(1, 0, 2).reshape(groups, -1)
    by_group = by_group[source_group[:, 0]].astype(bf16)[:, None, :]
    by_group = jnp.pad(by_group, ((0, 0), (0, TILE - 1), (0, width - servers * MOST)))
    parts = jnp.concatenate([d_tok_q, by_group], axis=1)
    parts = [parts[0]] + [ring(parts[k], -k) for k in range(1, groups)]
    d_tokens = from_quarters([part[:tok_dev] for part in parts], group, groups)

    mine = sum(part[tok_dev:tok_dev + 1, :servers * MOST].astype(f32) for part in parts)
    mine = mine + nil(grad_down)
    spot = chosen * MOST + order_rank
    match = spot[:, None] == jnp.arange(servers * MOST, dtype=jnp.int32)[None, :]
    d_gates = jnp.sum(jnp.where(match, mine, 0.0), axis=1).astype(bf16).reshape(tok_dev, top_count)
    return (
        d_tokens,
        d_gates,
        grad_both[0][None],
        grad_both[1][None],
        grad_down[None],
        load_here.reshape(1, 1),
    )


def solution(mesh):
    rows = P(("dp", "expert"), None)
    return jax.shard_map(
        shards,
        mesh=mesh,
        in_specs=(
            rows,
            rows,
            rows,
            rows,
            P("expert", "dp", None),
            P("expert", "dp", None),
            P("expert", None, "dp"),
            P(),
            rows,
        ),
        out_specs=(
            rows,
            rows,
            P("expert", "dp", None),
            P("expert", "dp", None),
            P("expert", None, "dp"),
            P("dp", "expert"),
        ),
        check_vma=False,
    )
```
